512 devices in a mesh: fsdp: 16 (over x, y_lo, core), ctx: 32 (over y_hi, z).
Axes of the slice: x: 4, y: 4 (y_hi: 2, y_lo: 2; y = y_hi * 2 + y_lo), z: 16, core: 2. Of those that a mesh axis runs over, the one named last changes fastest.
Arguments:
- qkv: bfloat16 [4096, 3, 8192], P('ctx', None, 'fsdp'), may hold values from -6 to 6
- short_filter: float32 [3, 7, 8192], P(None, None, 'fsdp'), may hold values from -2 to 2
- long_filter: float32 [128, 8192], P('ctx', 'fsdp'), may hold values from -0.5 to 0.5
- proj: bfloat16 [8192, 4096], P('fsdp', 'ctx'), may hold values from -0.125 to 0.125
- out_grad: bfloat16 [4096, 4096], P('ctx', 'fsdp'), may hold values from -6 to 6
Outputs:
- layer_out: bfloat16 [4096, 4096], P('ctx', 'fsdp')
- grad_qkv: bfloat16 [4096, 3, 8192], P('ctx', None, 'fsdp')
- grad_short: float32 [3, 7, 8192], P(None, None, 'fsdp')
- grad_long: float32 [128, 8192], P('ctx', 'fsdp')
- grad_proj: float32 [8192, 4096], P('fsdp', 'ctx')
The draws below stay inside these ranges and needn't reach their ends.
All inputs are finite; a program needn't handle non-finite values.
Results may differ from the reference program's by a relative error of at most 0.0049.
Values may be sent and summed in bfloat16 or wider, within the bound.
No kernel may reach another device: no remote copies, remote signals or barrier semaphores. Data moves between devices by JAX's collectives and lax.ppermute only.
A program may use at most 64 MiB of HBM per device.

```python
import jax
import jax.numpy as jnp
from jax import lax

D = 8192
DOUT = 4096
SHORT = 7
LTAPS = 128
TOKENS = 4096


def spiked(values, rng, source, target, shards_of, factor):
    def block_of(dim):
        return (jnp.arange(values.shape[dim]) // (values.shape[dim] // shards_of)).reshape((-1,) + (1,) * (values.ndim - 1 - dim))

    near = jax.random.permutation(rng, shards_of)[block_of(target)]
    second = (block_of(target) + shards_of // 2) % shards_of
    return jnp.where((block_of(source) == near) | (block_of(source) == second), factor * values, values)


def block_levels(key, shape, split, least, high):
    factor_of = 1.0
    for dim, parts in split:
        steps = jax.random.uniform(jax.random.fold_in(jax.random.fold_in(key, 6), dim), (parts,), jnp.float32, least / len(split), high / len(split))
        factor_of = factor_of * jnp.repeat(jnp.exp(steps), shape[dim] // parts).reshape((-1,) + (1,) * (len(shape) - 1 - dim))
    return factor_of


def centred(stream_key, extent, deviation, most, shards=(), held_as=jnp.bfloat16):
    drawn = jax.random.normal(stream_key, extent, jnp.float32) * deviation
    if len(shards) > 0:
        drawn = block_levels(stream_key, extent, shards, -0.22, 0.18) * drawn
    return jnp.clip(drawn, min=-most, max=most).astype(held_as)


def bell_draw_with(rng, shape, width, most, shards, heavy, kind=jnp.bfloat16):
    entries = width * jax.random.normal(rng, shape, jnp.float32)
    if shards:
        entries = entries * block_levels(rng, shape, shards, -0.22, 0.18)
    return jnp.clip(spiked(entries, jax.random.fold_in(rng, 3), *heavy), -most, most).astype(kind)


def setup_inputs(seed: int = 0) -> dict:
    key_of = jax.random.split(jax.random.key(seed), 6)
    return {
        "qkv": centred(key_of[0], (TOKENS, 3, D), 1.0, 6.0, ((0, 32), (2, 16))),
        "short_filter": centred(key_of[1], (3, SHORT, D), SHORT ** -0.5, 2.0, ((2, 16),), jnp.float32),
        "long_filter": centred(key_of[2], (LTAPS, D), LTAPS ** -0.5, 0.5, ((0, 32), (1, 16)), jnp.float32),
        "proj": bell_draw_with(key_of[3], (D, DOUT), D ** -0.5, 0.125, ((0, 16), (1, 32)), (0, 1, 32, 2.75)),
        "out_grad": centred(key_of[4], (TOKENS, DOUT), 1.0, 6.0, ((0, 32), (1, 16))),
    }


def causal_mix(series, taps):
    length = series.shape[0]
    span_taps = taps.shape[0]
    padded = jnp.concatenate([jnp.zeros((span_taps - 1, series.shape[1]), jnp.float32), series], axis=0)

    def add_tap(position, running):
        return running + taps[position] * lax.dynamic_slice_in_dim(padded, span_taps - 1 - position, length, 0)

    return lax.fori_loop(0, span_taps, add_tap, jnp.zeros(series.shape, jnp.float32))


def anticausal_mix(series, taps):
    length = series.shape[0]
    span_taps = taps.shape[0]
    padded = jnp.concatenate([series, jnp.zeros((span_taps - 1, series.shape[1]), jnp.float32)], axis=0)

    def add_tap(position, running):
        return running + taps[position] * lax.dynamic_slice_in_dim(padded, position, length, 0)

    return lax.fori_loop(0, span_taps, add_tap, jnp.zeros(series.shape, jnp.float32))


def tap_grads(series, grad_part, span_taps):
    length = series.shape[0]
    padded = jnp.concatenate([jnp.zeros((span_taps - 1, series.shape[1]), jnp.float32), series], axis=0)

    def one_tap(position):
        return jnp.sum(grad_part * lax.dynamic_slice_in_dim(padded, span_taps - 1 - position, length, 0), axis=0)

    return lax.map(one_tap, jnp.arange(span_taps, dtype=jnp.int32))


def reference(qkv, short_filter, long_filter, proj, out_grad):
    inputs = qkv.astype(jnp.float32).reshape(TOKENS, 3 * D)
    short_taps = jnp.transpose(short_filter, (1, 0, 2)).reshape(SHORT, 3 * D)
    short_out = causal_mix(inputs, short_taps)
    query_side = short_out[:, :D]
    key_side = short_out[:, D:2 * D]
    value_side = short_out[:, 2 * D:]
    product = key_side * value_side
    long_mix = causal_mix(product, long_filter)
    gated_out = (query_side * long_mix).astype(jnp.bfloat16)
    layer_out = jnp.dot(gated_out, proj, preferred_element_type=jnp.float32).astype(jnp.bfloat16)
    gated_grad = lax.dot_general(out_grad, proj, (((1,), (1,)), ((), ())), preferred_element_type=jnp.float32)
    grad_proj = lax.dot_general(gated_out, out_grad, (((0,), (0,)), ((), ())), preferred_element_type=jnp.float32)
    query_grad = gated_grad * long_mix
    mixed_grad = gated_grad * query_side
    product_grad = anticausal_mix(mixed_grad, long_filter)
    grad_long = tap_grads(product, mixed_grad, LTAPS)
    short_grad = jnp.concatenate([query_grad, product_grad * value_side, product_grad * key_side], axis=1)
    grad_inputs = anticausal_mix(short_grad, short_taps)
    grad_qkv = grad_inputs.reshape(TOKENS, 3, D).astype(jnp.bfloat16)
    grad_short = jnp.transpose(tap_grads(inputs, short_grad, SHORT).reshape(SHORT, 3, D), (1, 0, 2))
    return layer_out, grad_qkv, grad_short, grad_long, grad_proj
```

```python
import jax
import jax.numpy as jnp
from jax import lax
from jax.sharding import Mesh, PartitionSpec as P

F32 = jnp.float32
BF16 = jnp.bfloat16
AXES = ("x", "yl", "co", "yh", "z")
SIZES = (4, 2, 2, 2, 16)
CTX = ("yh", "z")
FSDP = ("x", "yl", "co")


def passed_along(value, steps):
    count = 32
    first, last = (max(0, -steps), min(count, count - steps))
    return lax.ppermute(value, CTX, [(source, source + steps) for source in range(first, last)])


def swapped(value, axis):
    return lax.ppermute(value, axis, [(0, 1), (1, 0)])


def ordered(index, own, other):
    first = jnp.where(index == 0, own, other)
    second = jnp.where(index == 0, other, own)
    return jnp.stack([first, second])


def depthwise(padded, kernel):
    result = lax.conv_general_dilated(
        padded[None],
        kernel[:, None, :],
        (1,),
        "VALID",
        dimension_numbers=("NWC", "WIO", "NWC"),
        feature_group_count=padded.shape[1],
        precision=lax.Precision.HIGHEST,
    )
    return result[0]


def owner_pairs():
    pairs = []
    for x in range(4):
        for rest in range(4):
            for yh in range(2):
                for z in range(16):
                    source = ((x * 4 + rest) * 2 + yh) * 16 + z
                    target = (((2 * yh + x % 2) * 4 + rest) * 2 + x // 2) * 16 + z
                    pairs.append((source, target))
    return pairs


def local(qkv, short_filter, long_filter, proj, out_grad):
    rows = qkv.shape[0]
    channels = qkv.shape[2]
    reach_short = short_filter.shape[1]
    taps_here = long_filter.shape[0]
    yh = lax.axis_index("yh")
    co = lax.axis_index("co")

    taps_high = lax.reduce_precision(long_filter, exponent_bits=8, mantissa_bits=7)
    taps_low = (long_filter - taps_high).astype(BF16)
    taps_high = taps_high.astype(BF16)
    pack_rows = 2 * taps_here * channels // 128
    pack = jnp.concatenate([taps_high, taps_low], axis=0).reshape(pack_rows, 128)
    gathered = lax.all_gather(jnp.concatenate([proj, pack], axis=0), "z", axis=1, tiled=True)
    proj_half = gathered[:channels]
    taps_pack = gathered[channels:].reshape(2, taps_here, channels // 128, 16, 128)
    taps_pack = jnp.transpose(taps_pack, (0, 3, 1, 2, 4)).reshape(2, 16 * taps_here, channels)
    taps_own = taps_pack[0].astype(F32) + taps_pack[1].astype(F32)
    taps_other = swapped(taps_own, "yh")
    long_taps = ordered(yh, taps_own, taps_other).reshape(32 * taps_here, channels)
    reach_long = long_taps.shape[0]

    along_x = lax.all_gather(out_grad, "x", axis=0, tiled=False).reshape(2, 2, rows, out_grad.shape[1])
    kept = lax.dynamic_index_in_dim(along_x, yh, 0, keepdims=False)
    given = lax.dynamic_index_in_dim(along_x, 1 - yh, 0, keepdims=False)
    both = ordered(yh, kept, swapped(given, "yh"))
    along_y = lax.all_gather(both, "yl", axis=0, tiled=False)
    along_c = ordered(co, along_y, swapped(along_y, "co"))
    grads = jnp.transpose(along_c, (2, 4, 3, 1, 0, 5)).reshape(2 * rows, 8 * out_grad.shape[1])

    inputs = qkv.reshape(rows, 3 * channels)
    input_rim = passed_along(inputs[rows - reach_short + 1 :], 1)
    extended = jnp.concatenate([input_rim, inputs], axis=0).astype(F32)
    short_taps = jnp.transpose(short_filter, (1, 0, 2)).reshape(reach_short, 3 * channels)
    short_out = depthwise(extended, short_taps[::-1])
    query_side = short_out[:, :channels]
    key_side = short_out[:, channels : 2 * channels]
    value_side = short_out[:, 2 * channels :]
    product = key_side * value_side
    product_rim = passed_along(product[rows - reach_long + 1 :], 1)
    product_ext = jnp.concatenate([product_rim, product], axis=0)

    grad_part = lax.dot_general(grads, proj_half, (((1,), (1,)), ((), ())), preferred_element_type=F32)
    grad_part = grad_part.reshape(2, rows, channels)
    part_kept = lax.dynamic_index_in_dim(grad_part, yh, 0, keepdims=False)
    part_given = lax.dynamic_index_in_dim(grad_part, 1 - yh, 0, keepdims=False)
    gated_grad = part_kept + swapped(part_given, "yh")

    long_mix = depthwise(product_ext, long_taps[::-1])
    gated_out = (query_side * long_mix).astype(BF16)
    gated_both = ordered(yh, gated_out, swapped(gated_out, "yh")).reshape(2 * rows, channels)

    out_part = jnp.dot(gated_both, proj_half, preferred_element_type=F32)
    out_part = out_part.reshape(2, rows, 2, 2, 2, out_grad.shape[1])
    out_part = jnp.transpose(out_part, (4, 0, 2, 3, 1, 5))
    out_kept = lax.dynamic_index_in_dim(out_part, co, 0, keepdims=False)
    out_given = lax.dynamic_index_in_dim(out_part, 1 - co, 0, keepdims=False)
    out_chip = (out_kept + swapped(out_given, "co")).astype(BF16).reshape(8, rows, out_grad.shape[1])
    out_terms = lax.all_to_all(out_chip, ("x", "yl"), 0, 0, tiled=True)
    out_sum = jnp.sum(out_terms.astype(F32), axis=0).astype(BF16)
    layer_out = lax.ppermute(out_sum, AXES, owner_pairs())

    proj_part = lax.dot_general(gated_both, grads, (((0,), (0,)), ((), ())), preferred_element_type=F32)
    grad_proj = lax.psum_scatter(proj_part, "z", scatter_dimension=1, tiled=True)

    query_grad = gated_grad * long_mix
    mixed_grad = gated_grad * query_side
    mixed_rim = passed_along(mixed_grad[: reach_long - 1], -1)
    product_grad = depthwise(jnp.concatenate([mixed_grad, mixed_rim], axis=0), long_taps)
    long_part = depthwise(product_ext, mixed_grad)[::-1].reshape(2, 16, taps_here, channels)
    short_grad = jnp.concatenate([query_grad, product_grad * value_side, product_grad * key_side], axis=1)
    short_rim = passed_along(short_grad[: reach_short - 1], -1)
    grad_inputs = depthwise(jnp.concatenate([short_grad, short_rim], axis=0), short_taps)
    grad_qkv = grad_inputs.reshape(rows, 3, channels).astype(BF16)
    short_part = depthwise(extended, short_grad)[::-1]

    short_rows = short_part.reshape(reach_short * 3, channels)
    short_rows = jnp.pad(short_rows, ((0, 32 - reach_short * 3), (0, 0))).reshape(16, 2, channels)
    long_kept = lax.dynamic_index_in_dim(long_part, yh, 0, keepdims=False)
    long_given = lax.dynamic_index_in_dim(long_part, 1 - yh, 0, keepdims=False)
    terms_given = jnp.concatenate([long_given, short_rows], axis=1)
    terms_kept = jnp.concatenate([long_kept, short_rows], axis=1)
    terms = terms_kept + swapped(terms_given, "yh")
    sums = jnp.sum(lax.all_to_all(terms, "z", 0, 0, tiled=True), axis=0)
    grad_long = sums[:taps_here]
    short_copies = jnp.broadcast_to(sums[None, taps_here:], (16, 2, channels))
    short_sum = lax.all_to_all(short_copies, "z", 0, 0, tiled=True).reshape(32, channels)[: 3 * reach_short]
    grad_short = jnp.transpose(short_sum.reshape(reach_short, 3, channels), (1, 0, 2))
    return (layer_out, grad_qkv, grad_short, grad_long, grad_proj)


def solution(mesh):
    fine = Mesh(mesh.devices.reshape(SIZES), AXES)
    in_specs = (
        P(CTX, None, FSDP),
        P(None, None, FSDP),
        P(CTX, FSDP),
        P(FSDP, CTX),
        P(CTX, FSDP),
    )
    out_specs = (
        P(CTX, FSDP),
        P(CTX, None, FSDP),
        P(None, None, FSDP),
        P(CTX, FSDP),
        P(FSDP, CTX),
    )
    return jax.shard_map(local, mesh=fine, in_specs=in_specs, out_specs=out_specs, check_vma=False)
```

```python
import jax
import jax.numpy as jnp
from jax import lax
from jax.experimental import pallas as pl
from jax.experimental.pallas import tpu as pltpu
from jax.sharding import Mesh, PartitionSpec as P

F32 = jnp.float32
BF16 = jnp.bfloat16
AXES = ("x", "yl", "co", "yh", "zh", "zl")
SIZES = (4, 2, 2, 2, 8, 2)
ALONG = ("zh", "zl")
CTX = ("yh", "zh", "zl")
FSDP = ("x", "yl", "co")
ROWS = 128
CHANNELS = 512
WIDE = 128
ZS = 16


def passed_along(value, steps):
    count = 32
    first, last = (max(0, -steps), min(count, count - steps))
    return lax.ppermute(value, CTX, [(source, source + steps) for source in range(first, last)])


def swapped(value, axis):
    return lax.ppermute(value, axis, [(0, 1), (1, 0)])


def ordered(index, own, other):
    first = jnp.where(index == 0, own, other)
    second = jnp.where(index == 0, other, own)
    return jnp.stack([first, second])


def after(value, *others):
    return lax.optimization_barrier((value, *others))[0]


def depthwise(padded, kernel):
    result = lax.conv_general_dilated(
        padded[None],
        kernel[:, None, :],
        (1,),
        "VALID",
        dimension_numbers=("NWC", "WIO", "NWC"),
        feature_group_count=padded.shape[1],
        precision=lax.Precision.HIGHEST,
    )
    return result[0]


def owner_pairs():
    pairs = []
    for x in range(4):
        for rest in range(4):
            for yh in range(2):
                for z in range(16):
                    source = ((x * 4 + rest) * 2 + yh) * 16 + z
                    target = (((2 * yh + x % 2) * 4 + rest) * 2 + x // 2) * 16 + z
                    pairs.append((source, target))
    return pairs


def gated_grad_kernel(yh_ref, grads_ref, proj_ref, kept_ref, given_ref):
    yh = yh_ref[0]

    def rows_of(block):
        total = jnp.zeros((ROWS, CHANNELS), F32)
        for z in range(ZS):
            total += lax.dot_general(
                grads_ref[z, pl.ds(pl.multiple_of(block * ROWS, ROWS), ROWS), :],
                proj_ref[z, :CHANNELS, :],
                (((1,), (1,)), ((), ())),
                preferred_element_type=F32,
            )
        return total

    given_ref[...] = rows_of(1 - yh).astype(BF16)
    kept_ref[...] = rows_of(yh)


def layer_out_kernel(gated_ref, proj_ref, out_ref):
    for z in range(ZS):
        terms = jnp.dot(gated_ref[...], proj_ref[z], preferred_element_type=F32).astype(BF16)
        columns = pl.ds((z % 2) * WIDE, WIDE)
        out_ref[z // 2, :, columns] = terms[:ROWS]
        out_ref[ZS // 2 + z // 2, :, columns] = terms[ROWS:]


def grad_proj_kernel(gated_ref, grads_ref, out_ref):
    for z in range(ZS):
        out_ref[z] = lax.dot_general(
            gated_ref[...], grads_ref[z], (((0,), (0,)), ((), ())), preferred_element_type=F32
        )


def call(kernel, outs, flops, args):
    specs = [
        pl.BlockSpec(memory_space=pltpu.SMEM if arg.ndim == 1 else pltpu.VMEM) for arg in args
    ]
    size = sum(arg.size * arg.dtype.itemsize for arg in args)
    size += sum(out.size * out.dtype.itemsize for out in outs)
    return pl.pallas_call(
        kernel,
        out_shape=outs,
        in_specs=specs,
        out_specs=[pl.BlockSpec(memory_space=pltpu.VMEM) for _ in outs],
        cost_estimate=pl.CostEstimate(flops=flops, bytes_accessed=size, transcendentals=0),
        compiler_params=pltpu.CompilerParams(vmem_limit_bytes=32 * 1024 * 1024),
    )(*args)


def shaped(shape, dtype):
    return jax.ShapeDtypeStruct(shape, dtype)


MATMUL = 2 * 256 * 512 * 2048


def local(qkv, short_filter, long_filter, proj, out_grad):
    rows = qkv.shape[0]
    channels = qkv.shape[2]
    reach_short = short_filter.shape[1]
    taps_here = long_filter.shape[0]
    yh = lax.axis_index("yh")
    co = lax.axis_index("co")

    gathered = lax.all_gather(proj, ALONG, axis=0, tiled=False)

    taps_pair = ordered(yh, long_filter, swapped(long_filter, "yh"))
    taps_copies = jnp.broadcast_to(taps_pair[None], (ZS,) + taps_pair.shape)
    taps_all = lax.all_to_all(taps_copies, ALONG, 0, 0, tiled=True)
    long_taps = jnp.transpose(taps_all, (1, 0, 2, 3)).reshape(2 * ZS * taps_here, channels)
    reach_long = long_taps.shape[0]

    copies = after(jnp.broadcast_to(out_grad[None], (ZS,) + out_grad.shape), taps_all)
    blocks = lax.all_to_all(copies, ("x", "yl", "yh"), 0, 0, tiled=True)
    blocks = blocks.reshape(2, 8, rows, 2 * WIDE)
    half = lax.dynamic_index_in_dim(blocks, yh, 0, keepdims=False)
    both = ordered(co, half, swapped(half, "co")).reshape(2, 2, 2, 2, rows, 2, WIDE)
    grads = jnp.transpose(both, (1, 2, 0, 5, 3, 4, 6)).reshape(ZS, 2 * rows, WIDE)

    inputs = qkv.reshape(rows, 3 * channels)
    reach = reach_short - 1
    sent = jnp.concatenate([inputs[:, channels:], inputs[rows - 8 :, :channels].reshape(4, 2 * channels)], axis=0)
    before = passed_along(sent, 1)
    far = passed_along(inputs[rows - 8 :, channels:], 2)
    query_rim = before[rows:].reshape(8, channels)[8 - reach :]
    before = before[:rows]
    rim = jnp.concatenate([query_rim, before[rows - reach :]], axis=1)
    extended = jnp.concatenate([rim, inputs], axis=0).astype(F32)
    short_taps = jnp.transpose(short_filter, (1, 0, 2)).reshape(reach_short, 3 * channels)
    query_side = depthwise(extended[:, :channels], short_taps[::-1, :channels])
    pairs = jnp.concatenate([far[8 - reach :], before, inputs[:, channels:]], axis=0)
    pairs = depthwise(pairs.astype(F32), short_taps[::-1, channels:])
    key_side = pairs[rows:, :channels]
    value_side = pairs[rows:, channels:]
    product_ext = (pairs[:, :channels] * pairs[:, channels:])[2 * rows - (rows + reach_long - 1) :]

    long_mix = depthwise(product_ext, long_taps[::-1])
    gated_out = (query_side * long_mix).astype(BF16)
    gated_both = ordered(yh, gated_out, swapped(gated_out, "yh")).reshape(2 * rows, channels)

    (proj_part,) = call(
        grad_proj_kernel, [shaped((ZS, channels, WIDE), F32)], MATMUL, [gated_both, grads]
    )
    grad_proj = lax.psum_scatter(
        proj_part.reshape(ZS * channels, WIDE), ALONG, scatter_dimension=0, tiled=True
    )

    gathered = after(gathered, proj_part)

    part_kept, part_given = call(
        gated_grad_kernel,
        [shaped((rows, channels), F32), shaped((rows, channels), BF16)],
        MATMUL,
        [yh.reshape(1), grads, gathered],
    )
    gated_grad = part_kept + swapped(part_given, "yh").astype(F32)

    (out_part,) = call(
        layer_out_kernel,
        [shaped((ZS, rows, 2 * WIDE), BF16)],
        MATMUL,
        [after(gated_both, proj_part), gathered],
    )
    out_terms = lax.all_to_all(out_part, FSDP, 0, 0, tiled=True)

    query_grad = gated_grad * long_mix
    mixed_grad = gated_grad * query_side
    mixed_rim = passed_along(mixed_grad.astype(BF16), -1).astype(F32)[: reach_long - 1]
    long_part = depthwise(product_ext, mixed_grad)[::-1].reshape(2, ZS, taps_here, channels)
    mixed_ext = jnp.concatenate([mixed_grad, after(mixed_rim, out_part, long_part)], axis=0)
    product_grad = depthwise(mixed_ext, long_taps)
    short_grad = jnp.concatenate([query_grad, product_grad * value_side, product_grad * key_side], axis=1)
    short_rim = passed_along(short_grad[: reach_short - 1], -1)
    grad_inputs = depthwise(jnp.concatenate([short_grad, short_rim], axis=0), short_taps)
    grad_qkv = grad_inputs.reshape(rows, 3, channels).astype(BF16)
    short_part = depthwise(extended, short_grad)[::-1]

    short_rows = jnp.pad(short_part.reshape(3 * reach_short, channels), ((0, 3), (0, 0)))
    long_kept = lax.dynamic_index_in_dim(long_part, yh, 0, keepdims=False)
    long_given = lax.dynamic_index_in_dim(long_part, 1 - yh, 0, keepdims=False)
    terms_given = jnp.concatenate([long_given.reshape(ZS * taps_here, channels), short_rows], axis=0)
    terms_got = swapped(terms_given, "yh")
    long_half = long_kept + terms_got[: ZS * taps_here].reshape(long_kept.shape)
    short_pair = (short_rows + terms_got[ZS * taps_here :]).astype(BF16)
    short_pair, out_terms, long_half = lax.optimization_barrier((short_pair, out_terms, long_half))
    grad_long = jnp.sum(lax.all_to_all(long_half, ALONG, 0, 0, tiled=True), axis=0)

    out_sum = jnp.sum(out_terms.astype(F32), axis=0).astype(BF16)
    layer_out = lax.ppermute(out_sum, AXES, owner_pairs())

    short_sum = jnp.sum(lax.all_gather(short_pair, ALONG, axis=0, tiled=False).astype(F32), axis=0)
    grad_short = jnp.transpose(short_sum[: 3 * reach_short].reshape(reach_short, 3, channels), (1, 0, 2))
    return (layer_out, grad_qkv, grad_short, grad_long, grad_proj)


def solution(mesh):
    fine = Mesh(mesh.devices.reshape(SIZES), AXES)
    in_specs = (
        P(CTX, None, FSDP),
        P(None, None, FSDP),
        P(CTX, FSDP),
        P(FSDP, CTX),
        P(CTX, FSDP),
    )
    out_specs = (
        P(CTX, FSDP),
        P(CTX, None, FSDP),
        P(None, None, FSDP),
        P(CTX, FSDP),
        P(FSDP, CTX),
    )
    return jax.shard_map(local, mesh=fine, in_specs=in_specs, out_specs=out_specs, check_vma=False)
```

```python
import jax
import jax.numpy as jnp
from jax import lax
from jax.experimental import pallas as pl
from jax.experimental.pallas import tpu as pltpu
from jax.sharding import Mesh, PartitionSpec as P

F32 = jnp.float32
BF16 = jnp.bfloat16
AXES = ("x", "yl", "co", "yh", "zh", "zl")
SIZES = (4, 2, 2, 2, 8, 2)
ALONG = ("zh", "zl")
CTX = ("yh", "zh", "zl")
FSDP = ("x", "yl", "co")
ROWS = 128
CHANNELS = 512
WIDE = 128
ZS = 16


def passed_along(value, steps):
    count = 32
    first, last = (max(0, -steps), min(count, count - steps))
    return lax.ppermute(value, CTX, [(source, source + steps) for source in range(first, last)])


def swapped(value, axis):
    return lax.ppermute(value, axis, [(0, 1), (1, 0)])


def ordered(index, own, other):
    first = jnp.where(index == 0, own, other)
    second = jnp.where(index == 0, other, own)
    return jnp.stack([first, second])


def after(value, *others):
    return lax.optimization_barrier((value, *others))[0]


def depthwise(padded, kernel):
    result = lax.conv_general_dilated(
        padded[None],
        kernel[:, None, :],
        (1,),
        "VALID",
        dimension_numbers=("NWC", "WIO", "NWC"),
        feature_group_count=padded.shape[1],
        precision=lax.Precision.HIGHEST,
    )
    return result[0]


def owner_pairs():
    pairs = []
    for x in range(4):
        for rest in range(4):
            for yh in range(2):
                for z in range(16):
                    source = ((x * 4 + rest) * 2 + yh) * 16 + z
                    target = (((2 * yh + x % 2) * 4 + rest) * 2 + x // 2) * 16 + z
                    pairs.append((source, target))
    return pairs


def gated_grad_kernel(yh_ref, grads_ref, proj_ref, kept_ref, given_ref):
    yh = yh_ref[0]

    def rows_of(block):
        total = jnp.zeros((ROWS, CHANNELS), F32)
        for z in range(ZS):
            total += lax.dot_general(
                grads_ref[z, pl.ds(pl.multiple_of(block * ROWS, ROWS), ROWS), :],
                proj_ref[z, :CHANNELS, :],
                (((1,), (1,)), ((), ())),
                preferred_element_type=F32,
            )
        return total

    given_ref[...] = rows_of(1 - yh).astype(BF16)
    kept_ref[...] = rows_of(yh)


def layer_out_kernel(gated_ref, proj_ref, out_ref):
    for z in range(ZS):
        terms = jnp.dot(gated_ref[...], proj_ref[z], preferred_element_type=F32).astype(BF16)
        columns = pl.ds((z % 2) * WIDE, WIDE)
        out_ref[z // 2, :, columns] = terms[:ROWS]
        out_ref[ZS // 2 + z // 2, :, columns] = terms[ROWS:]


def grad_proj_kernel(gated_ref, grads_ref, out_ref):
    for z in range(ZS):
        out_ref[z] = lax.dot_general(
            gated_ref[...], grads_ref[z], (((0,), (0,)), ((), ())), preferred_element_type=F32
        )


def call(kernel, outs, flops, args):
    specs = [
        pl.BlockSpec(memory_space=pltpu.SMEM if arg.ndim == 1 else pltpu.VMEM) for arg in args
    ]
    size = sum(arg.size * arg.dtype.itemsize for arg in args)
    size += sum(out.size * out.dtype.itemsize for out in outs)
    return pl.pallas_call(
        kernel,
        out_shape=outs,
        in_specs=specs,
        out_specs=[pl.BlockSpec(memory_space=pltpu.VMEM) for _ in outs],
        cost_estimate=pl.CostEstimate(flops=flops, bytes_accessed=size, transcendentals=0),
        compiler_params=pltpu.CompilerParams(vmem_limit_bytes=32 * 1024 * 1024),
    )(*args)


def shaped(shape, dtype):
    return jax.ShapeDtypeStruct(shape, dtype)


MATMUL = 2 * 256 * 512 * 2048


def local(qkv, short_filter, long_filter, proj, out_grad):
    rows = qkv.shape[0]
    channels = qkv.shape[2]
    reach_short = short_filter.shape[1]
    taps_here = long_filter.shape[0]
    yh = lax.axis_index("yh")
    co = lax.axis_index("co")

    inputs = qkv.reshape(rows, 3 * channels)
    reach = reach_short - 1
    input_rim = passed_along(inputs[rows - reach :], 1)

    gathered = lax.all_gather(proj, ALONG, axis=0, tiled=False)

    taps_pair = ordered(yh, long_filter, swapped(long_filter, "yh"))
    taps_copies = jnp.broadcast_to(taps_pair[None], (ZS,) + taps_pair.shape)
    taps_copies = after(taps_copies, input_rim)
    taps_all = lax.all_to_all(taps_copies, ALONG, 0, 0, tiled=True)
    long_taps = jnp.transpose(taps_all, (1, 0, 2, 3)).reshape(2 * ZS * taps_here, channels)
    reach_long = long_taps.shape[0]

    copies = after(jnp.broadcast_to(out_grad[None], (ZS,) + out_grad.shape), taps_all)
    blocks = lax.all_to_all(copies, ("x", "yl", "yh"), 0, 0, tiled=True)
    blocks = blocks.reshape(2, 8, rows, 2 * WIDE)
    half = lax.dynamic_index_in_dim(blocks, yh, 0, keepdims=False)
    both = ordered(co, half, swapped(half, "co")).reshape(2, 2, 2, 2, rows, 2, WIDE)
    grads = jnp.transpose(both, (1, 2, 0, 5, 3, 4, 6)).reshape(ZS, 2 * rows, WIDE)

    extended = jnp.concatenate([input_rim, inputs], axis=0).astype(F32)
    short_taps = jnp.transpose(short_filter, (1, 0, 2)).reshape(reach_short, 3 * channels)
    short_out = depthwise(extended, short_taps[::-1])
    query_side = short_out[:, :channels]
    key_side = short_out[:, channels : 2 * channels]
    value_side = short_out[:, 2 * channels :]
    product = key_side * value_side
    product_rim = passed_along(product[rows - reach_long + 1 :], 1)
    product_ext = jnp.concatenate([product_rim, product], axis=0)

    long_mix = depthwise(product_ext, long_taps[::-1])
    gated_out = (query_side * long_mix).astype(BF16)
    gated_both = ordered(yh, gated_out, swapped(gated_out, "yh")).reshape(2 * rows, channels)

    (proj_part,) = call(
        grad_proj_kernel, [shaped((ZS, channels, WIDE), F32)], MATMUL, [gated_both, grads]
    )
    grad_proj = lax.psum_scatter(
        proj_part.reshape(ZS * channels, WIDE), ALONG, scatter_dimension=0, tiled=True
    )

    gathered = after(gathered, proj_part)

    part_kept, part_given = call(
        gated_grad_kernel,
        [shaped((rows, channels), F32), shaped((rows, channels), BF16)],
        MATMUL,
        [yh.reshape(1), grads, gathered],
    )
    gated_grad = part_kept + swapped(part_given, "yh").astype(F32)

    (out_part,) = call(
        layer_out_kernel,
        [shaped((ZS, rows, 2 * WIDE), BF16)],
        MATMUL,
        [after(gated_both, proj_part), gathered],
    )
    out_terms = lax.all_to_all(out_part, FSDP, 0, 0, tiled=True)

    query_grad = gated_grad * long_mix
    mixed_grad = gated_grad * query_side
    mixed_rim = passed_along(mixed_grad.astype(BF16), -1).astype(F32)[: reach_long - 1]
    long_part = depthwise(product_ext, mixed_grad)[::-1].reshape(2, ZS, taps_here, channels)
    mixed_ext = jnp.concatenate([mixed_grad, after(mixed_rim, out_part, long_part)], axis=0)
    product_grad = depthwise(mixed_ext, long_taps)
    short_grad = jnp.concatenate([query_grad, product_grad * value_side, product_grad * key_side], axis=1)
    short_part = depthwise(extended, short_grad)[::-1]
    short_rim = passed_along(after(short_grad[: reach_short - 1], short_part), -1)
    grad_inputs = depthwise(jnp.concatenate([short_grad, short_rim], axis=0), short_taps)
    grad_qkv = grad_inputs.reshape(rows, 3, channels).astype(BF16)

    short_rows = jnp.pad(short_part.reshape(3 * reach_short, channels), ((0, 32 - 3 * reach_short), (0, 0)))
    short_rows = short_rows.reshape(ZS, 2, channels)
    long_kept = lax.dynamic_index_in_dim(long_part, yh, 0, keepdims=False)
    long_given = lax.dynamic_index_in_dim(long_part, 1 - yh, 0, keepdims=False)
    terms_got = swapped(jnp.concatenate([long_given, short_rows], axis=1).astype(BF16), "yh")
    terms = jnp.concatenate([long_kept, short_rows], axis=1) + terms_got.astype(F32)
    terms = terms.astype(BF16)
    terms, out_terms = lax.optimization_barrier((terms, out_terms))
    sums = jnp.sum(lax.all_to_all(terms, ALONG, 0, 0, tiled=True).astype(F32), axis=0)
    grad_long = sums[:taps_here]
    short_copies = jnp.broadcast_to(sums[None, taps_here:], (ZS, 2, channels))
    short_sum = lax.all_to_all(short_copies, ALONG, 0, 0, tiled=True).reshape(2 * ZS, channels)
    grad_short = jnp.transpose(short_sum[: 3 * reach_short].reshape(reach_short, 3, channels), (1, 0, 2))

    out_sum = jnp.sum(out_terms.astype(F32), axis=0).astype(BF16)
    layer_out = lax.ppermute(out_sum, AXES, owner_pairs())
    return (layer_out, grad_qkv, grad_short, grad_long, grad_proj)


def solution(mesh):
    fine = Mesh(mesh.devices.reshape(SIZES), AXES)
    in_specs = (
        P(CTX, None, FSDP),
        P(None, None, FSDP),
        P(CTX, FSDP),
        P(FSDP, CTX),
        P(CTX, FSDP),
    )
    out_specs = (
        P(CTX, FSDP),
        P(CTX, None, FSDP),
        P(None, None, FSDP),
        P(CTX, FSDP),
        P(FSDP, CTX),
    )
    return jax.shard_map(local, mesh=fine, in_specs=in_specs, out_specs=out_specs, check_vma=False)
```

```python
import jax
import jax.numpy as jnp
from jax import lax
from jax.experimental import pallas as pl
from jax.experimental.pallas import tpu as pltpu
from jax.sharding import Mesh, PartitionSpec as P

F32 = jnp.float32
BF16 = jnp.bfloat16
AXES = ("x", "yl", "co", "yh", "zh", "zl")
SIZES = (4, 2, 2, 2, 8, 2)
ALONG = ("zh", "zl")
CTX = ("yh", "zh", "zl")
FSDP = ("x", "yl", "co")
ROWS = 128
CHANNELS = 512
WIDE = 128
ZS = 16


def passed_along(value, steps):
    count = 32
    first, last = (max(0, -steps), min(count, count - steps))
    return lax.ppermute(value, CTX, [(source, source + steps) for source in range(first, last)])


def swapped(value, axis):
    return lax.ppermute(value, axis, [(0, 1), (1, 0)])


def ordered(index, own, other):
    first = jnp.where(index == 0, own, other)
    second = jnp.where(index == 0, other, own)
    return jnp.stack([first, second])


def after(value, *others):
    return lax.optimization_barrier((value, *others))[0]


def depthwise(padded, kernel):
    result = lax.conv_general_dilated(
        padded[None],
        kernel[:, None, :],
        (1,),
        "VALID",
        dimension_numbers=("NWC", "WIO", "NWC"),
        feature_group_count=padded.shape[1],
        precision=lax.Precision.HIGHEST,
    )
    return result[0]


def owner_pairs():
    pairs = []
    for x in range(4):
        for rest in range(4):
            for yh in range(2):
                for z in range(16):
                    source = ((x * 4 + rest) * 2 + yh) * 16 + z
                    target = (((2 * yh + x % 2) * 4 + rest) * 2 + x // 2) * 16 + z
                    pairs.append((source, target))
    return pairs


def gated_grad_kernel(yh_ref, grads_ref, proj_ref, kept_ref, given_ref):
    yh = yh_ref[0]

    def rows_of(block):
        total = jnp.zeros((ROWS, CHANNELS), F32)
        for z in range(ZS):
            total += lax.dot_general(
                grads_ref[z, pl.ds(pl.multiple_of(block * ROWS, ROWS), ROWS), :],
                proj_ref[z, :CHANNELS, :],
                (((1,), (1,)), ((), ())),
                preferred_element_type=F32,
            )
        return total

    given_ref[...] = rows_of(1 - yh).astype(BF16)
    kept_ref[...] = rows_of(yh)


def layer_out_kernel(gated_ref, proj_ref, out_ref):
    for z in range(ZS):
        terms = jnp.dot(gated_ref[...], proj_ref[z], preferred_element_type=F32).astype(BF16)
        columns = pl.ds((z % 2) * WIDE, WIDE)
        out_ref[z // 2, :, columns] = terms[:ROWS]
        out_ref[ZS // 2 + z // 2, :, columns] = terms[ROWS:]


def grad_proj_kernel(gated_ref, grads_ref, out_ref):
    for z in range(ZS):
        out_ref[z] = lax.dot_general(
            gated_ref[...], grads_ref[z], (((0,), (0,)), ((), ())), preferred_element_type=F32
        )


def call(kernel, outs, flops, args):
    specs = [
        pl.BlockSpec(memory_space=pltpu.SMEM if arg.ndim == 1 else pltpu.VMEM) for arg in args
    ]
    size = sum(arg.size * arg.dtype.itemsize for arg in args)
    size += sum(out.size * out.dtype.itemsize for out in outs)
    return pl.pallas_call(
        kernel,
        out_shape=outs,
        in_specs=specs,
        out_specs=[pl.BlockSpec(memory_space=pltpu.VMEM) for _ in outs],
        cost_estimate=pl.CostEstimate(flops=flops, bytes_accessed=size, transcendentals=0),
        compiler_params=pltpu.CompilerParams(vmem_limit_bytes=32 * 1024 * 1024),
    )(*args)


def shaped(shape, dtype):
    return jax.ShapeDtypeStruct(shape, dtype)


MATMUL = 2 * 256 * 512 * 2048


def local(qkv, short_filter, long_filter, proj, out_grad):
    rows = qkv.shape[0]
    channels = qkv.shape[2]
    reach_short = short_filter.shape[1]
    taps_here = long_filter.shape[0]
    yh = lax.axis_index("yh")
    co = lax.axis_index("co")

    inputs = qkv.reshape(rows, 3 * channels)
    reach = reach_short - 1
    input_rim = passed_along(inputs[rows - reach :], 1)

    gathered = lax.all_gather(proj, ALONG, axis=0, tiled=False)

    taps_pair = ordered(yh, long_filter, swapped(long_filter, "yh"))
    taps_copies = jnp.broadcast_to(taps_pair[None], (ZS,) + taps_pair.shape)
    taps_copies = after(taps_copies, input_rim)
    taps_all = lax.all_to_all(taps_copies, ALONG, 0, 0, tiled=True)
    long_taps = jnp.transpose(taps_all, (1, 0, 2, 3)).reshape(2 * ZS * taps_here, channels)
    reach_long = long_taps.shape[0]

    copies = after(jnp.broadcast_to(out_grad[None], (ZS,) + out_grad.shape), taps_all)
    blocks = lax.all_to_all(copies, ("x", "yl", "yh"), 0, 0, tiled=True)
    blocks = blocks.reshape(2, 8, rows, 2 * WIDE)
    half = lax.dynamic_index_in_dim(blocks, yh, 0, keepdims=False)
    both = ordered(co, half, swapped(half, "co")).reshape(2, 2, 2, 2, rows, 2, WIDE)
    grads = jnp.transpose(both, (1, 2, 0, 5, 3, 4, 6)).reshape(ZS, 2 * rows, WIDE)

    extended = jnp.concatenate([input_rim, inputs], axis=0).astype(F32)
    short_taps = jnp.transpose(short_filter, (1, 0, 2)).reshape(reach_short, 3 * channels)
    short_out = depthwise(extended, short_taps[::-1])
    query_side = short_out[:, :channels]
    key_side = short_out[:, channels : 2 * channels]
    value_side = short_out[:, 2 * channels :]
    product = key_side * value_side
    product_rim = passed_along(product[rows - reach_long + 1 :], 1)
    product_ext = jnp.concatenate([product_rim, product], axis=0)

    long_mix = depthwise(product_ext, long_taps[::-1])
    gated_out = (query_side * long_mix).astype(BF16)
    gated_both = ordered(yh, gated_out, swapped(gated_out, "yh")).reshape(2 * rows, channels)

    (proj_part,) = call(
        grad_proj_kernel, [shaped((ZS, channels, WIDE), F32)], MATMUL, [gated_both, grads]
    )
    grad_proj = lax.psum_scatter(
        proj_part.reshape(ZS * channels, WIDE), ALONG, scatter_dimension=0, tiled=True
    )

    gathered = after(gathered, proj_part)

    part_kept, part_given = call(
        gated_grad_kernel,
        [shaped((rows, channels), F32), shaped((rows, channels), BF16)],
        MATMUL,
        [yh.reshape(1), grads, gathered],
    )
    gated_grad = part_kept + swapped(part_given, "yh").astype(F32)

    query_grad = gated_grad * long_mix
    mixed_grad = gated_grad * query_side
    mixed_rim = passed_along(mixed_grad.astype(BF16), -1).astype(F32)[: reach_long - 1]

    (out_part,) = call(
        layer_out_kernel,
        [shaped((ZS, rows, 2 * WIDE), BF16)],
        MATMUL,
        [after(gated_both, mixed_grad), gathered],
    )
    out_terms = lax.all_to_all(out_part, FSDP, 0, 0, tiled=True)

    long_part = depthwise(product_ext, mixed_grad)[::-1].reshape(2, ZS, taps_here, channels)
    mixed_ext = jnp.concatenate([mixed_grad, after(mixed_rim, out_part, long_part)], axis=0)
    product_grad = depthwise(mixed_ext, long_taps)
    short_grad = jnp.concatenate([query_grad, product_grad * value_side, product_grad * key_side], axis=1)
    short_part = depthwise(extended, short_grad)[::-1]
    short_rim = passed_along(after(short_grad[: reach_short - 1], short_part), -1)
    grad_inputs = depthwise(jnp.concatenate([short_grad, short_rim], axis=0), short_taps)
    grad_qkv = grad_inputs.reshape(rows, 3, channels).astype(BF16)

    short_rows = jnp.pad(short_part.reshape(3 * reach_short, channels), ((0, 32 - 3 * reach_short), (0, 0)))
    short_rows = short_rows.reshape(ZS, 2, channels)
    long_kept = lax.dynamic_index_in_dim(long_part, yh, 0, keepdims=False)
    long_given = lax.dynamic_index_in_dim(long_part, 1 - yh, 0, keepdims=False)
    terms_got = swapped(jnp.concatenate([long_given, short_rows], axis=1).astype(BF16), "yh")
    terms = jnp.concatenate([long_kept, short_rows], axis=1) + terms_got.astype(F32)
    terms = terms.astype(BF16)
    terms, out_terms = lax.optimization_barrier((terms, out_terms))
    sums = jnp.sum(lax.all_to_all(terms, ALONG, 0, 0, tiled=True).astype(F32), axis=0)
    grad_long = sums[:taps_here]
    out_sum = jnp.sum(out_terms.astype(F32), axis=0).astype(BF16)
    layer_out = lax.ppermute(out_sum, AXES, owner_pairs())
    short_copies = jnp.broadcast_to(sums[None, taps_here:].astype(BF16), (ZS, 2, channels))
    short_copies = after(short_copies, out_sum, grad_qkv)
    short_sum = lax.all_to_all(short_copies, ALONG, 0, 0, tiled=True).astype(F32).reshape(2 * ZS, channels)
    grad_short = jnp.transpose(short_sum[: 3 * reach_short].reshape(reach_short, 3, channels), (1, 0, 2))
    return (layer_out, grad_qkv, grad_short, grad_long, grad_proj)


def solution(mesh):
    fine = Mesh(mesh.devices.reshape(SIZES), AXES)
    in_specs = (
        P(CTX, None, FSDP),
        P(None, None, FSDP),
        P(CTX, FSDP),
        P(FSDP, CTX),
        P(CTX, FSDP),
    )
    out_specs = (
        P(CTX, FSDP),
        P(CTX, None, FSDP),
        P(None, None, FSDP),
        P(CTX, FSDP),
        P(FSDP, CTX),
    )
    return jax.shard_map(local, mesh=fine, in_specs=in_specs, out_specs=out_specs, check_vma=False)
```
